32 devices in a mesh: seq: 8 (over z, x), head: 4 (over y, core).
Axes of the slice: x: 2, y: 2, z: 4, core: 2. Of those that a mesh axis runs over, the one named last changes fastest.
Arguments:
- queries: bfloat16 [8192, 5120], P('seq', 'head')
- keys: bfloat16 [8192, 5120], P('seq', 'head')
- values: bfloat16 [8192, 5120], P('seq', 'head'), may hold values from -6 to 6
- query_gain: float32 [5120], P('head'), may hold values from 0.1 to 1.9
- key_gain: float32 [5120], P('head'), may hold values from 0.1 to 1.9
- shapes: int32 [2, 3], replicated, may hold values from 4 to 32, as said below
- windows: int32 [64, 27], P('seq'), may hold values from -1 to 63, as said below
- text_keys: bfloat16 [8, 256, 5120], P(None, 'seq', 'head')
- text_values: bfloat16 [8, 256, 5120], P(None, 'seq', 'head'), may hold values from -6 to 6
- owner: int32 [2], replicated, may hold values from 0 to 7, as said below
Outputs:
- attended: bfloat16 [8192, 5120], P('seq', 'head')
The draws below stay inside these ranges and needn't reach their ends.
Inputs may be any that keep to these rules, and one draw needn't show every extreme that they name: `shapes`: row s is (frames, height, width) of video s in tokens: height and width are 16 and 32, or 32 and 16, so a frame has 4 tiles; each video has from 16 to 48 tiles, and the videos' tiles add up to 64, so no tile holds tokens of two videos. `windows`: entry k of row g stands for the tile k // 9 - 1 frames, (k // 3) % 3 - 1 tile rows and k % 3 - 1 tile columns away from tile g in its video: it holds that tile's number or -1; it is -1 wherever that tile lies outside the video, and entry 13 is always g. `owner`: no two videos share a panel.
All inputs are finite; a program needn't handle non-finite values.
Results may differ from the reference program's by a relative error of at most 0.012.
Values may be sent and summed in bfloat16 or wider, within the bound.
No kernel may reach another device: no remote copies, remote signals or barrier semaphores. Data moves between devices by JAX's collectives and lax.ppermute only.
A program may use at most 192 MiB of HBM per device.

```python
import jax
import jax.numpy as jnp
from jax import lax

HEAD_DIM = 128
HEADS = 40
D = 5120
TILE_H = 8
TILE_W = 16
TILE = 128
WIN = 27
REACH = 7
TXT = 256
TILES_DEV = 8
TOKENS = 8192
NTILES = 64
SAMPLES = 2
PANELS = 8


def sample_shapes(key):
    half_count = SAMPLES // 2
    units = jax.random.randint(jax.random.fold_in(key, 11), (half_count,), TILES_DEV // 2, 3 * TILES_DEV // 2 + 1)
    units = units.at[0].set(3 * TILES_DEV // 2)
    partner = jax.random.permutation(jax.random.fold_in(key, 12), half_count)
    tile_counts = 4 * jnp.concatenate([units, 2 * TILES_DEV - units[partner]])
    shuffle = jax.random.permutation(jax.random.fold_in(key, 13), SAMPLES)
    tile_counts = tile_counts[shuffle]
    landscape = jax.random.randint(jax.random.fold_in(key, 14), (SAMPLES,), 0, 2) == 1
    landscape = jnp.where(tile_counts == 6 * TILES_DEV, True, jnp.where(tile_counts == 2 * TILES_DEV, False, landscape))
    row_counts = jnp.where(landscape, 2, 4)
    col_counts = jnp.where(landscape, 2, 1)
    frame_counts = tile_counts // 4
    return jnp.stack([frame_counts, row_counts * TILE_H, col_counts * TILE_W], axis=1).astype(jnp.int32)


def draw_shapes(key, part):
    return sample_shapes(key)


def draw_windows(key, part):
    shape_rows = sample_shapes(key)
    row_counts = shape_rows[:, 1] // TILE_H
    col_counts = shape_rows[:, 2] // TILE_W
    tile_counts = shape_rows[:, 0] * row_counts * col_counts
    tile_ends = jnp.cumsum(tile_counts).astype(jnp.int32)
    tile_starts = tile_ends - tile_counts
    tile_ids = jnp.arange(NTILES, dtype=jnp.int32)
    sample_ids = jnp.sum((tile_ids[:, None] >= tile_ends[None, :]).astype(jnp.int32), axis=1)
    first_tiles = tile_starts[sample_ids]
    rows_here = row_counts[sample_ids]
    cols_here = col_counts[sample_ids]
    frame_counts = shape_rows[sample_ids, 0]
    offsets = tile_ids - first_tiles
    per_frame = rows_here * cols_here
    frames = offsets // per_frame
    within = offsets % per_frame
    bands = within // cols_here
    columns = within % cols_here
    slots = jnp.arange(WIN, dtype=jnp.int32)
    time_step = slots // 9 - 1
    band_step = slots // 3 % 3 - 1
    column_step = slots % 3 - 1
    near_frame = frames[:, None] + time_step[None, :]
    near_band = bands[:, None] + band_step[None, :]
    near_column = columns[:, None] + column_step[None, :]
    inside = (near_frame >= 0) & (near_frame < frame_counts[:, None]) & (near_band >= 0) & (near_band < rows_here[:, None]) & (near_column >= 0) & (near_column < cols_here[:, None])
    chosen = jax.random.randint(jax.random.fold_in(key, 21), (NTILES, WIN), 0, 2) == 1
    chosen = chosen | ((time_step == 0) & (band_step == 0) & (column_step == 0))[None, :]
    near_ids = first_tiles[:, None] + near_frame * per_frame[:, None] + near_band * cols_here[:, None] + near_column
    return jnp.where(inside & chosen, near_ids, -1).astype(jnp.int32)


def feature_field(key):
    columns = jnp.arange(D, dtype=jnp.float32) / D
    rough = jnp.exp(jax.random.uniform(jax.random.fold_in(key, 31), (D,), minval=-0.35, maxval=0.35))
    column_scale = 3.0 ** (0.5 * columns) * rough
    row_scale = jnp.exp(jax.random.uniform(jax.random.fold_in(key, 32), (TOKENS, 1), minval=0.0, maxval=2.31))
    entries = jax.random.normal(jax.random.fold_in(key, 33), (TOKENS, D), dtype=jnp.float32)
    return entries * row_scale * column_scale[None, :]


def draw_queries(key, part):
    return feature_field(jax.random.fold_in(key, 41)).astype(jnp.bfloat16)


def draw_keys(key, part):
    return feature_field(jax.random.fold_in(key, 42)).astype(jnp.bfloat16)


def draw_text_keys(key, part):
    inner_key = jax.random.fold_in(key, 51)
    entries = jax.random.normal(inner_key, (PANELS, TXT, D), dtype=jnp.float32)
    return entries.astype(jnp.bfloat16)


def draw_owner(key, part):
    others = jax.random.permutation(jax.random.fold_in(key, 61), PANELS - 1)[:SAMPLES - 1].astype(jnp.int32)
    chosen = jnp.concatenate([others, jnp.full((1,), PANELS - 1, dtype=jnp.int32)])
    order = jax.random.permutation(jax.random.fold_in(key, 62), SAMPLES)
    return chosen[order].astype(jnp.int32)


def level_of(own_key, shape, pieces, least, high):
    level, own = 1.0, jax.random.fold_in(own_key, 6)
    for axis_at, shards_of in pieces:
        steps = jnp.exp(jax.random.uniform(jax.random.fold_in(own, axis_at), (shards_of,), jnp.float32, least / len(pieces), high / len(pieces)))
        level = level * jnp.repeat(steps, shape[axis_at] // shards_of).reshape([-1 if axis == axis_at else 1 for axis in range(len(shape))])
    return level


def noise(key, dims, deviation, reach, pieces=(), kind=jnp.bfloat16):
    drawn = deviation * jax.random.normal(key, dims, jnp.float32)
    if pieces:
        drawn = drawn * level_of(key, dims, pieces, -0.22, 0.18)
    return jnp.clip(drawn, -reach, reach).astype(kind)


def setup_inputs(seed: int = 0) -> dict:
    splits = jax.random.split(jax.random.key(seed), 11)
    return {
        "queries": draw_queries(jax.random.fold_in(splits[10], 71), 0),
        "keys": draw_keys(jax.random.fold_in(splits[10], 71), 0),
        "values": noise(splits[2], (TOKENS, D), 1.0, 6.0, ((0, 8), (1, 4))),
        "query_gain": jnp.clip(1.0 + 0.18 * jax.random.normal(splits[3], (D,), jnp.float32), 0.1, 1.9),
        "key_gain": jnp.clip(1.0 + 0.18 * jax.random.normal(splits[4], (D,), jnp.float32), 0.1, 1.9),
        "shapes": draw_shapes(jax.random.fold_in(splits[10], 71), 0),
        "windows": draw_windows(jax.random.fold_in(splits[10], 71), 0),
        "text_keys": draw_text_keys(jax.random.fold_in(splits[10], 71), 0),
        "text_values": noise(splits[8], (PANELS, TXT, D), 1.0, 6.0, ((1, 8), (2, 4))),
        "owner": draw_owner(jax.random.fold_in(splits[10], 71), 0),
    }


epsilon = 1e-06

def tile_table(shape_rows):
    per_frame = shape_rows[:, 1] // TILE_H * (shape_rows[:, 2] // TILE_W)
    tile_counts = shape_rows[:, 0] * per_frame
    tile_ends = jnp.cumsum(tile_counts).astype(jnp.int32)
    return ((tile_ends - tile_counts).astype(jnp.int32), tile_ends)

def locate(tile_ids, shape_rows, tile_starts, tile_ends):
    sample_ids = lax.optimization_barrier(jnp.sum((tile_ids[:, None] >= tile_ends[None, :]).astype(jnp.int32), axis=1)).astype(jnp.int32)
    one_hot = (sample_ids[:, None] == jnp.arange(tile_ends.shape[0], dtype=jnp.int32)[None, :]).astype(jnp.int32)
    first_tiles = lax.optimization_barrier(jnp.sum(one_hot * tile_starts[None, :], axis=1)).astype(jnp.int32)
    row_counts = lax.optimization_barrier(jnp.sum(one_hot * (shape_rows[:, 1] // TILE_H)[None, :], axis=1)).astype(jnp.int32)
    col_counts = lax.optimization_barrier(jnp.sum(one_hot * (shape_rows[:, 2] // TILE_W)[None, :], axis=1)).astype(jnp.int32)
    offsets = tile_ids - first_tiles
    per_frame = row_counts * col_counts
    within = offsets % per_frame
    return (sample_ids, one_hot, offsets // per_frame, within // col_counts, within % col_counts)

def rope_angles(frames, bands, columns, head_size):
    inner = jnp.arange(TILE_H * TILE_W, dtype=jnp.int32)
    tile_total = frames.shape[0]
    time_pos = jnp.broadcast_to(frames[:, None], (tile_total, inner.shape[0])).reshape(-1).astype(jnp.float32)
    row_pos = (bands[:, None] * TILE_H + inner[None, :] // TILE_W).reshape(-1).astype(jnp.float32)
    col_pos = (columns[:, None] * TILE_W + inner[None, :] % TILE_W).reshape(-1).astype(jnp.float32)
    third = head_size // 6
    part_sizes = (head_size - 4 * third, 2 * third, 2 * third)
    angle_parts = []
    for position, part_size in zip((time_pos, row_pos, col_pos), part_sizes):
        frequency = 10000.0 ** (-jnp.arange(0, part_size, 2, dtype=jnp.float32) / part_size)
        angle_parts.append(position[:, None] * frequency[None, :])
    return jnp.concatenate(angle_parts, axis=1)

def rotate(field, angles):
    paired = field.reshape(field.shape[0], field.shape[1], field.shape[2] // 2, 2)
    cosine = jnp.cos(angles)[:, None, :]
    sine = jnp.sin(angles)[:, None, :]
    even_part = paired[..., 0]
    odd_part = paired[..., 1]
    turned = jnp.stack([even_part * cosine - odd_part * sine, even_part * sine + odd_part * cosine], axis=-1)
    return turned.reshape(field.shape)

def reference(queries, keys, values, query_gain, key_gain, shapes, windows, text_keys, text_values, owner):
    tile_starts, tile_ends = tile_table(shapes)
    tile_ids = jnp.arange(NTILES, dtype=jnp.int32)
    sample_ids, one_hot, frames, bands, columns = locate(tile_ids, shapes, tile_starts, tile_ends)
    panel_ids = lax.optimization_barrier(jnp.sum(one_hot * owner[None, :], axis=1)).astype(jnp.int32)

    def make_prepare(gain):

        def prepare(items):
            block_rows, frame_one, band_one, column_one = items
            angles = rope_angles(frame_one[None], band_one[None], column_one[None], HEAD_DIM)
            widened = block_rows.astype(jnp.float32)
            scaled = widened * lax.rsqrt(lax.optimization_barrier(jnp.mean(widened * widened, axis=1, keepdims=True)) + epsilon) * gain[None, :]
            return rotate(scaled.reshape(TILE, HEADS, HEAD_DIM), angles).astype(jnp.bfloat16)
        return prepare
    q_hat = lax.map(make_prepare(query_gain), (queries.reshape(NTILES, TILE, D), frames, bands, columns)).reshape(TOKENS, HEADS, HEAD_DIM)
    k_hat = lax.map(make_prepare(key_gain), (keys.reshape(NTILES, TILE, D), frames, bands, columns)).reshape(TOKENS, HEADS, HEAD_DIM)
    margin = REACH * TILE
    k_padded = jnp.pad(k_hat, ((margin, margin), (0, 0), (0, 0)))
    v_padded = jnp.pad(values.reshape(TOKENS, HEADS, HEAD_DIM), ((margin, margin), (0, 0), (0, 0)))
    span_rows = (2 * REACH + 1) * TILE
    factor = HEAD_DIM ** (-0.5)

    def attend(tile_index):
        query_rows = lax.dynamic_slice_in_dim(q_hat, tile_index * TILE, TILE, 0).astype(jnp.float32)
        key_rows = lax.dynamic_slice_in_dim(k_padded, tile_index * TILE, span_rows, 0)
        value_rows = lax.dynamic_slice_in_dim(v_padded, tile_index * TILE, span_rows, 0)
        panel = lax.dynamic_index_in_dim(panel_ids, tile_index, 0, keepdims=False)
        prompt_keys = lax.dynamic_index_in_dim(text_keys, panel, 0, keepdims=False).reshape(TXT, HEADS, HEAD_DIM)
        prompt_values = lax.dynamic_index_in_dim(text_values, panel, 0, keepdims=False).reshape(TXT, HEADS, HEAD_DIM)
        key_tiles = tile_index - REACH + jnp.arange(2 * REACH + 1, dtype=jnp.int32)
        listed = lax.dynamic_index_in_dim(windows, tile_index, 0, keepdims=False)
        allowed = jnp.any(listed[:, None] == key_tiles[None, :], axis=0) & (key_tiles >= 0)
        key_mask = jnp.concatenate([jnp.repeat(allowed, TILE), jnp.ones((TXT,), dtype=bool)])
        all_keys = jnp.concatenate([key_rows, prompt_keys], axis=0).astype(jnp.float32)
        all_values = jnp.concatenate([value_rows, prompt_values], axis=0).astype(jnp.float32)
        scores = jnp.einsum('qhd,khd->hqk', query_rows, all_keys) * factor
        scores = jnp.where(key_mask[None, None, :], scores, -jnp.inf)
        largest = lax.optimization_barrier(jnp.max(scores, axis=-1, keepdims=True))
        weights = jnp.exp(scores - largest)
        totals = lax.optimization_barrier(jnp.sum(weights, axis=-1))
        rounded = lax.optimization_barrier(weights.astype(jnp.bfloat16))
        mixed = jnp.einsum('hqk,khd->qhd', rounded.astype(jnp.float32), all_values)
        mixed = mixed / jnp.transpose(totals)[:, :, None]
        return mixed.astype(jnp.bfloat16).reshape(TILE, D)
    return lax.map(attend, tile_ids).reshape(TOKENS, D)
```

```python
import functools
import math

import jax
import jax.numpy as jnp
import numpy as np
from jax import lax
from jax.experimental import pallas as pl
from jax.experimental.pallas import tpu as pltpu
from jax.sharding import PartitionSpec as P

HEAD_DIM = 128
D = 5120
TILE_H = 8
TILE_W = 16
TILE = 128
FRAME_TILES = 4
FRAME = FRAME_TILES * TILE
TXT = 256
EPSILON = 1e-06
OUT_OF_WINDOW = -1e30


def tile_positions(tile_ids, shapes):
    per_frame = shapes[:, 1] // TILE_H * (shapes[:, 2] // TILE_W)
    tile_counts = shapes[:, 0] * per_frame
    tile_ends = jnp.cumsum(tile_counts)
    tile_starts = tile_ends - tile_counts
    sample_ids = jnp.sum((tile_ids[:, None] >= tile_ends[None, :]).astype(jnp.int32), axis=1)
    one_hot = (
        sample_ids[:, None] == jnp.arange(shapes.shape[0], dtype=jnp.int32)[None, :]
    ).astype(jnp.int32)
    first_tiles = jnp.sum(one_hot * tile_starts[None, :], axis=1)
    row_counts = jnp.sum(one_hot * (shapes[:, 1] // TILE_H)[None, :], axis=1)
    col_counts = jnp.sum(one_hot * (shapes[:, 2] // TILE_W)[None, :], axis=1)
    offsets = tile_ids - first_tiles
    per_tile = row_counts * col_counts
    within = offsets % per_tile
    return sample_ids, offsets // per_tile, within // col_counts, within % col_counts


def lane_tables():
    third = HEAD_DIM // 6
    part_sizes = (HEAD_DIM - 4 * third, 2 * third, 2 * third)
    part = np.concatenate([np.full(size, at) for at, size in enumerate(part_sizes)])
    pair_at = np.concatenate([np.arange(size) // 2 * 2 for size in part_sizes])
    size_at = np.concatenate([np.full(size, size) for size in part_sizes])
    return part, pair_at.astype(np.float32), size_at.astype(np.float32)


def rotation(frames, bands, columns):
    part, pair_at, size_at = lane_tables()
    inner = jnp.arange(TILE, dtype=jnp.int32)
    tiles = frames.shape[0]
    time_pos = jnp.broadcast_to(frames[:, None], (tiles, TILE)).reshape(-1, 1)
    row_pos = (bands[:, None] * TILE_H + inner[None, :] // TILE_W).reshape(-1, 1)
    col_pos = (columns[:, None] * TILE_W + inner[None, :] % TILE_W).reshape(-1, 1)
    lane_part = jnp.asarray(part, jnp.int32)[None, :]
    position = jnp.where(lane_part == 0, time_pos, jnp.where(lane_part == 1, row_pos, col_pos))
    frequency = 10000.0 ** (-jnp.asarray(pair_at) / jnp.asarray(size_at))
    angles = position.astype(jnp.float32) * frequency[None, :]
    sign = jnp.asarray(np.where(np.arange(HEAD_DIM) % 2 == 0, -1.0, 1.0), jnp.float32)
    return jnp.cos(angles), jnp.sin(angles) * sign[None, :]


def head_sum(partial):
    count = lax.axis_size("head")
    if count & (count - 1):
        return lax.psum(partial, "head")
    step = 1
    while step < count:
        partial = partial + lax.ppermute(partial, "head", [(i, i ^ step) for i in range(count)])
        step *= 2
    return partial


def turn_kernel(x_ref, cos_ref, sin_ref, gain_ref, swapped_gain_ref, o_ref):
    x = x_ref[...]
    row = lax.broadcasted_iota(jnp.int32, (HEAD_DIM, HEAD_DIM), 0)
    col = lax.broadcasted_iota(jnp.int32, (HEAD_DIM, HEAD_DIM), 1)
    exchange = (row == col + 1 - 2 * (col % 2)).astype(jnp.bfloat16)
    swapped = jnp.dot(x, exchange, preferred_element_type=jnp.float32)
    turned = (x.astype(jnp.float32) * gain_ref[...]) * cos_ref[...]
    turned += (swapped * swapped_gain_ref[...]) * sin_ref[...]
    o_ref[...] = turned.astype(jnp.bfloat16)


def turn(field, cosine, sine, gain):
    rows, width = field.shape
    heads = width // HEAD_DIM
    swapped_gain = gain.reshape(-1, 2)[:, ::-1].reshape(1, width)
    column = pl.BlockSpec((rows, HEAD_DIM), lambda h: (0, h))
    table = pl.BlockSpec((rows, HEAD_DIM), lambda h: (0, 0))
    line = pl.BlockSpec((1, HEAD_DIM), lambda h: (0, h))
    return pl.pallas_call(
        turn_kernel,
        grid=(heads,),
        in_specs=[column, table, table, line, line],
        out_specs=column,
        out_shape=jax.ShapeDtypeStruct((rows, width), jnp.bfloat16),
        compiler_params=pltpu.CompilerParams(vmem_limit_bytes=24 * 2**20),
        cost_estimate=pl.CostEstimate(
            flops=2 * rows * width * HEAD_DIM, bytes_accessed=4 * rows * width, transcendentals=0
        ),
    )(field, cosine, sine, gain.reshape(1, width), swapped_gain)


def attend_kernel(meta_ref, q_ref, k_ref, v_ref, kn_ref, vn_ref, tk_ref, tv_ref, *rest):
    o_ref, key_ref, val_ref, s_ref, p_ref = rest[-5:]
    own, near = k_ref.shape[0], kn_ref.shape[0]
    total = own + near + TXT

    @pl.when(pl.program_id(0) == 0)
    def _():
        val_ref[:, HEAD_DIM:] = jnp.ones((total, HEAD_DIM), jnp.bfloat16)

    key_ref[:own, :] = k_ref[...]
    key_ref[own : own + near, :] = kn_ref[...]
    key_ref[own + near :, :] = tk_ref[...]
    val_ref[:own, :HEAD_DIM] = v_ref[...]
    val_ref[own : own + near, :HEAD_DIM] = vn_ref[...]
    val_ref[own + near :, :HEAD_DIM] = tv_ref[...]
    window_tiles = (own + near) // TILE
    key_tiles = total // TILE
    for i in range(FRAME_TILES):
        rows = slice(i * TILE, (i + 1) * TILE)
        s_ref[rows, :] = lax.dot_general(
            q_ref[rows, :],
            key_ref[...],
            (((1,), (1,)), ((), ())),
            preferred_element_type=jnp.float32,
        )
        bias = [
            jnp.where(meta_ref[1 + i * window_tiles + j] == 0, OUT_OF_WINDOW, 0.0)
            for j in range(window_tiles)
        ]
        largest = None
        for j in range(key_tiles):
            part = s_ref[rows, j * TILE : (j + 1) * TILE]
            if j < window_tiles:
                part = part + bias[j]
            largest = part if largest is None else jnp.maximum(largest, part)
        largest = jnp.max(largest, axis=1, keepdims=True)
        for j in range(key_tiles):
            cols = slice(j * TILE, (j + 1) * TILE)
            top = largest - bias[j] if j < window_tiles else largest
            p_ref[rows, cols] = jnp.exp2(s_ref[rows, cols] - top).astype(jnp.bfloat16)
        mixed = jnp.dot(p_ref[rows, :], val_ref[...], preferred_element_type=jnp.float32)
        o_ref[rows, :] = (mixed[:, :HEAD_DIM] / mixed[:, HEAD_DIM:]).astype(jnp.bfloat16)


def attend(meta, q_hat, k_hat, values, near_k, near_v, text, place, first, heads, out=None):
    rows, width = q_hat.shape
    total = rows + FRAME + TXT

    def own(h, meta):
        return (0, first + h)

    frame_block = pl.BlockSpec((FRAME, HEAD_DIM), lambda h, meta: (meta[0], first + h))
    near_spec = pl.BlockSpec((None, FRAME, HEAD_DIM), lambda h, meta: (0, 0, h))
    near_spec_v = pl.BlockSpec(
        (None, FRAME, HEAD_DIM), lambda h, meta: (near_v.shape[0] - 1, 0, h)
    )
    text_specs = [
        pl.BlockSpec((None, None, TXT, HEAD_DIM), lambda h, meta, at=at: (at, place, 0, first + h))
        for at in range(2)
    ]
    in_specs = [
        frame_block,
        pl.BlockSpec((rows, HEAD_DIM), own),
        pl.BlockSpec((rows, HEAD_DIM), own),
        near_spec,
        near_spec_v,
        *text_specs,
    ]
    operands = [q_hat, k_hat, values, near_k, near_v, text, text]
    aliases = {}
    if out is not None:
        in_specs.append(pl.BlockSpec(memory_space=pl.ANY))
        operands.append(out)
        aliases = {len(operands): 0}
    return pl.pallas_call(
        attend_kernel,
        grid_spec=pltpu.PrefetchScalarGridSpec(
            num_scalar_prefetch=1,
            grid=(heads,),
            in_specs=in_specs,
            out_specs=frame_block,
            scratch_shapes=[
                pltpu.VMEM((total, HEAD_DIM), jnp.bfloat16),
                pltpu.VMEM((total, 2 * HEAD_DIM), jnp.bfloat16),
                pltpu.VMEM((FRAME, total), jnp.float32),
                pltpu.VMEM((FRAME, total), jnp.bfloat16),
            ],
        ),
        out_shape=jax.ShapeDtypeStruct((rows, width), jnp.bfloat16),
        input_output_aliases=aliases,
        compiler_params=pltpu.CompilerParams(vmem_limit_bytes=32 * 2**20),
        cost_estimate=pl.CostEstimate(
            flops=heads * FRAME * total * HEAD_DIM * 8,
            bytes_accessed=heads * (2 * total + 2 * FRAME) * HEAD_DIM * 2,
            transcendentals=heads * FRAME * total,
        ),
    )(meta, *operands)


def after(value, *others):
    return lax.optimization_barrier((value, *others))[0]


def local(
    queries, keys, values, query_gain, key_gain, shapes, windows, text_keys, text_values, owner
):
    rows, width = queries.shape
    heads = width // HEAD_DIM
    tiles = rows // TILE
    count = lax.axis_size("seq")
    me = lax.axis_index("seq")
    odd = me % 2
    first_tile = me * tiles
    pair = [(i, i ^ 1) for i in range(count)]
    side = [p for i in range(1, count - 1, 2) for p in ((i, i + 1), (i + 1, i))]
    pair_frame, side_frame = 1 - odd, odd

    chosen = jnp.stack([jnp.take(text_keys, owner, axis=0), jnp.take(text_values, owner, axis=0)])
    both = jnp.concatenate([chosen, lax.ppermute(chosen, "seq", pair)], axis=2)
    pair_values = lax.dynamic_slice_in_dim(values, pair_frame * FRAME, FRAME, 0)[None]
    near_values = lax.ppermute(pair_values, "seq", pair)
    if count <= 8:
        text = jnp.concatenate(
            [both]
            + [
                lax.ppermute(both, "seq", [(i, (i + 2 * k) % count) for i in range(count)])
                for k in range(1, count // 2)
            ],
            axis=2,
        )
    else:
        groups = [list(range(start, count, 2)) for start in range(2)]
        text = lax.all_gather(both, "seq", axis=2, tiled=True, axis_index_groups=groups)

    tile_ids = first_tile + jnp.arange(tiles, dtype=jnp.int32)
    sample_ids, frames, bands, columns = tile_positions(tile_ids, shapes)
    cosine, sine = rotation(frames, bands, columns)
    query_wide = queries.astype(jnp.float32)
    key_wide = keys.astype(jnp.float32)
    squares = head_sum(
        jnp.stack([jnp.sum(query_wide * query_wide, axis=1), jnp.sum(key_wide * key_wide, axis=1)])
    )
    scale = lax.rsqrt(squares / D + EPSILON)
    key_scale = scale[1][:, None]
    query_scale = scale[0][:, None] * (HEAD_DIM**-0.5 * math.log2(math.e))
    k_hat = turn(keys, cosine * key_scale, sine * key_scale, key_gain)
    pair_keys = lax.dynamic_slice_in_dim(k_hat, pair_frame * FRAME, FRAME, 0)[None]
    near_keys = lax.ppermute(pair_keys, "seq", pair)
    q_hat = turn(queries, cosine * query_scale, sine * query_scale, query_gain)

    step = 2 if heads % 2 == 0 else 1
    side_keys = lax.dynamic_slice_in_dim(k_hat, side_frame * FRAME, FRAME, 0)
    side_values = lax.dynamic_slice_in_dim(values, side_frame * FRAME, FRAME, 0)
    arrived = [near_values, near_keys]
    for start in range(0, heads, step):
        cols = slice(start * HEAD_DIM, (start + step) * HEAD_DIM)
        parcel = jnp.stack([side_keys[:, cols], side_values[:, cols]])
        arrived.append(lax.ppermute(after(parcel, arrived[-2]), "seq", side))
    side_parcels = arrived[2:]

    own_ids = tile_ids.reshape(2, FRAME_TILES)
    frame_windows = windows.reshape(2, FRAME_TILES, windows.shape[1])
    frame_samples = sample_ids.reshape(2, FRAME_TILES)[:, 0]
    order = jnp.stack([pair_frame, side_frame])
    slots = jnp.take(frame_samples, order)
    text = jnp.take(text, slots, axis=1)
    before_ids = own_ids[0] - FRAME_TILES
    after_ids = own_ids[1] + FRAME_TILES

    def meta_of(frame):
        near_ids = jnp.where(frame == 0, before_ids, after_ids)
        key_ids = jnp.concatenate([own_ids[0], own_ids[1], near_ids])
        listed = jnp.take(frame_windows, frame, axis=0)
        allowed = jnp.any(listed[:, :, None] == key_ids[None, None, :], axis=1) & (key_ids >= 0)
        return jnp.concatenate([frame[None], allowed.astype(jnp.int32).reshape(-1)])

    out = attend(
        meta_of(pair_frame), q_hat, k_hat, values, near_keys, near_values, text, 0, 0, heads
    )
    meta = meta_of(side_frame)
    for at, parcel in enumerate(side_parcels):
        out = attend(
            meta, q_hat, k_hat, values, parcel, parcel, text, 1, at * step, step, out
        )
    return out


def solution(mesh):
    placed = (
        P("seq", "head"),
        P("seq", "head"),
        P("seq", "head"),
        P("head"),
        P("head"),
        P(),
        P("seq", None),
        P(None, "seq", "head"),
        P(None, "seq", "head"),
        P(),
    )
    return jax.shard_map(
        local, mesh=mesh, in_specs=placed, out_specs=P("seq", "head"), check_vma=False
    )
```

```python
import functools
import math

import jax
import jax.numpy as jnp
import numpy as np
from jax import lax
from jax.experimental import pallas as pl
from jax.experimental.pallas import tpu as pltpu
from jax.sharding import PartitionSpec as P

HEAD_DIM = 128
D = 5120
TILE_H = 8
TILE_W = 16
TILE = 128
FRAME_TILES = 4
FRAME = FRAME_TILES * TILE
TXT = 256
WIN = 27
EPSILON = 1e-06
OUT_OF_WINDOW = -1e30
SMALL = pl.CostEstimate(flops=1000, bytes_accessed=1000, transcendentals=0)


def cost(heads, rows, keys):
    return pl.CostEstimate(
        flops=8 * heads * rows * keys * HEAD_DIM,
        bytes_accessed=6 * heads * rows * keys,
        transcendentals=heads * rows * keys,
    )


def lane_tables():
    third = HEAD_DIM // 6
    part_sizes = (HEAD_DIM - 4 * third, 2 * third, 2 * third)
    part = np.concatenate([np.full(size, at) for at, size in enumerate(part_sizes)])
    pair_at = np.concatenate([np.arange(size) // 2 * 2 for size in part_sizes])
    size_at = np.concatenate([np.full(size, size) for size in part_sizes])
    frequency = 10000.0 ** (-jnp.asarray(pair_at, jnp.float32) / jnp.asarray(size_at, jnp.float32))
    return jnp.asarray(part, jnp.int32)[None, :], frequency[None, :]


def plan_kernel(samples, me_ref, shapes_ref, windows_ref, place_ref, own_ref, pair_ref, side_ref):
    me = me_ref[0]
    tiles = 2 * FRAME_TILES
    first = me * tiles
    odd = lax.rem(me, 2)
    narrow = []
    for f in range(2):
        frame_at = first + f * FRAME_TILES
        start, own_start, sample = 0, 0, 0
        single = shapes_ref[2] == TILE_W
        for s in range(samples):
            if s:
                inside = frame_at >= start
                sample = jnp.where(inside, s, sample)
                own_start = jnp.where(inside, start, own_start)
                single = jnp.where(inside, shapes_ref[3 * s + 2] == TILE_W, single)
            start = start + FRAME_TILES * shapes_ref[3 * s]
        narrow.append(single)
        moment = (frame_at - own_start) // FRAME_TILES
        for a in range(FRAME_TILES):
            at = 3 * (f * FRAME_TILES + a)
            place_ref[at] = moment
            place_ref[at + 1] = jnp.where(single, a, a // 2)
            place_ref[at + 2] = jnp.where(single, 0, a % 2)
        is_pair = odd == 1 - f
        for ref, wanted in ((pair_ref, is_pair), (side_ref, jnp.logical_not(is_pair))):

            @pl.when(wanted)
            def _(ref=ref, f=f, sample=sample):
                ref[0] = f
                ref[1] = sample

    def flag(f, a, step, b):
        tall = (step + 1) * 9 + (b - a + 1) * 3 + 1
        square = (step + 1) * 9 + (b // 2 - a // 2 + 1) * 3 + b % 2 - a % 2 + 1
        row = (f * FRAME_TILES + a) * WIN
        key = first + (f + step) * FRAME_TILES + b
        if abs(b - a) > 1:
            found = jnp.logical_and(jnp.logical_not(narrow[f]), windows_ref[row + square] == key)
        else:
            found = windows_ref[row + jnp.where(narrow[f], tall, square)] == key
        return jnp.logical_and(found, key >= 0).astype(jnp.int32)

    for f in range(2):
        near_step = 2 * f - 1
        near = [flag(f, a, near_step, b) for a in range(FRAME_TILES) for b in range(FRAME_TILES)]
        is_pair = odd == 1 - f
        for ref, wanted in ((pair_ref, is_pair), (side_ref, jnp.logical_not(is_pair))):

            @pl.when(wanted)
            def _(ref=ref, near=near):
                for at, value in enumerate(near):
                    ref[2 + at] = value

        for a in range(FRAME_TILES):
            for g in range(2):
                for b in range(FRAME_TILES):
                    at = (f * FRAME_TILES + a) * tiles + g * FRAME_TILES + b
                    own_ref[at] = flag(f, a, g - f, b)


def plan(me, shapes, windows):
    samples = shapes.shape[0]
    tiles = 2 * FRAME_TILES
    smem = pl.BlockSpec(memory_space=pltpu.SMEM)
    sizes = (3 * tiles, tiles * tiles, 2 + FRAME_TILES**2, 2 + FRAME_TILES**2)
    return pl.pallas_call(
        functools.partial(plan_kernel, samples),
        in_specs=[smem] * 3,
        out_specs=[smem] * 4,
        out_shape=[jax.ShapeDtypeStruct((size,), jnp.int32) for size in sizes],
        cost_estimate=SMALL,
    )(me.reshape(1), shapes.reshape(-1), windows.reshape(-1))


def head_sum(partial):
    count = lax.axis_size("head")
    if count & (count - 1):
        return lax.psum(partial, "head")
    step = 1
    while step < count:
        partial = partial + lax.ppermute(partial, "head", [(i, i ^ step) for i in range(count)])
        step *= 2
    return partial


def exchange_pairs(row):
    lane = lax.broadcasted_iota(jnp.int32, row.shape, 1)
    return jnp.where(lane % 2 == 0, pltpu.roll(row, HEAD_DIM - 1, 1), pltpu.roll(row, 1, 1))


def turn_kernel(place_ref, part_ref, frequency_ref, squares_ref, *refs):
    fields, gains, outs, tables = refs[:2], refs[2:4], refs[4:6], refs[6:]
    rows, width = fields[0].shape

    @pl.when(pl.program_id(0) == 0)
    def _():
        token = lax.broadcasted_iota(jnp.int32, (TILE, HEAD_DIM), 0)
        lane = lax.broadcasted_iota(jnp.int32, (TILE, HEAD_DIM), 1)
        part = part_ref[...]
        for i in range(rows // TILE):
            time_pos, band, column = (place_ref[3 * i + axis] for axis in range(3))
            row_pos = band * TILE_H + token // TILE_W
            col_pos = column * TILE_W + token % TILE_W
            position = jnp.where(part == 0, time_pos, jnp.where(part == 1, row_pos, col_pos))
            angles = position.astype(jnp.float32) * frequency_ref[...]
            cosine = jnp.cos(angles)
            sine = jnp.sin(angles) * jnp.where(lane % 2 == 0, -1.0, 1.0)
            at = slice(i * TILE, (i + 1) * TILE)
            for n, factor in enumerate((HEAD_DIM**-0.5 * math.log2(math.e), 1.0)):
                scale = lax.rsqrt(squares_ref[n : n + 1, at] / D + EPSILON) * factor
                scale = jnp.transpose(jnp.broadcast_to(scale, (TILE, HEAD_DIM)))
                tables[2 * n][at, :] = cosine * scale
                tables[2 * n + 1][at, :] = sine * scale

    row = lax.broadcasted_iota(jnp.int32, (HEAD_DIM, HEAD_DIM), 0)
    col = lax.broadcasted_iota(jnp.int32, (HEAD_DIM, HEAD_DIM), 1)
    exchange = (row == col + 1 - 2 * (col % 2)).astype(jnp.bfloat16)
    for n in range(2):
        for u in range(width // HEAD_DIM):
            cols = slice(u * HEAD_DIM, (u + 1) * HEAD_DIM)
            x = fields[n][:, cols]
            gain = jnp.broadcast_to(gains[n][:, cols], (8, HEAD_DIM))
            swapped = jnp.dot(x, exchange, preferred_element_type=jnp.float32)
            turned = (x.astype(jnp.float32) * gain[:1]) * tables[2 * n][...]
            turned += (swapped * exchange_pairs(gain)[:1]) * tables[2 * n + 1][...]
            outs[n][:, cols] = turned.astype(jnp.bfloat16)


def turn(place, squares, queries, keys, query_gain, key_gain):
    rows, width = queries.shape
    heads = width // HEAD_DIM
    step = 2 - heads % 2
    part, frequency = lane_tables()
    column = pl.BlockSpec((rows, step * HEAD_DIM), lambda h, place: (0, h))
    line = pl.BlockSpec((1, step * HEAD_DIM), lambda h, place: (0, h))
    lanes = pl.BlockSpec((1, HEAD_DIM), lambda h, place: (0, 0))
    whole = pl.BlockSpec((2, rows), lambda h, place: (0, 0))
    return pl.pallas_call(
        turn_kernel,
        grid_spec=pltpu.PrefetchScalarGridSpec(
            num_scalar_prefetch=1,
            grid=(heads // step,),
            in_specs=[lanes, lanes, whole, column, column, line, line],
            out_specs=[column, column],
            scratch_shapes=[pltpu.VMEM((rows, HEAD_DIM), jnp.float32) for _ in range(4)],
        ),
        out_shape=[jax.ShapeDtypeStruct((rows, width), jnp.bfloat16)] * 2,
        compiler_params=pltpu.CompilerParams(vmem_limit_bytes=24 * 2**20),
        cost_estimate=SMALL,
    )(
        place,
        part,
        frequency,
        squares,
        queries,
        keys,
        query_gain.reshape(1, width),
        key_gain.reshape(1, width),
    )


def choose_kernel(owner_ref, keys_ref, values_ref, o_ref):
    o_ref[0] = keys_ref[...]
    o_ref[1] = values_ref[...]


def choose(owner, text_keys, text_values):
    panels, rows, width = text_keys.shape
    samples = owner.shape[0]
    panel = pl.BlockSpec((None, rows, width), lambda s, owner: (owner[s], 0, 0))
    return pl.pallas_call(
        choose_kernel,
        grid_spec=pltpu.PrefetchScalarGridSpec(
            num_scalar_prefetch=1,
            grid=(samples,),
            in_specs=[panel, panel],
            out_specs=pl.BlockSpec((2, None, rows, width), lambda s, owner: (0, s, 0, 0)),
        ),
        out_shape=jax.ShapeDtypeStruct((2, samples, rows, width), text_keys.dtype),
        cost_estimate=SMALL,
    )(owner, text_keys, text_values)


def attend_blocks(heads, tiles, query, keys, bias, val_ref, s_ref, p_ref, floor_of, finish):
    def score(u, i):
        rows = slice(i * TILE, (i + 1) * TILE)
        s_ref[u, rows, :] = lax.dot_general(
            query(u, rows),
            keys(u),
            (((1,), (1,)), ((), ())),
            preferred_element_type=jnp.float32,
        )

    def weigh(u, i):
        rows = slice(i * TILE, (i + 1) * TILE)
        largest = None
        for j in range(s_ref.shape[2] // TILE):
            part = s_ref[u, rows, j * TILE : (j + 1) * TILE]
            if j < len(bias[i]):
                part = part + bias[i][j]
            largest = part if largest is None else jnp.maximum(largest, part)
        largest = jnp.max(largest, axis=1, keepdims=True)
        floor = floor_of(u, rows)
        if floor is None:
            largest = jnp.broadcast_to(largest, (TILE, HEAD_DIM))
        else:
            largest = jnp.maximum(largest, floor)
        for j in range(s_ref.shape[2] // TILE):
            cols = slice(j * TILE, (j + 1) * TILE)
            top = largest - bias[i][j] if j < len(bias[i]) else largest
            p_ref[u, rows, cols] = jnp.exp2(s_ref[u, rows, cols] - top).astype(jnp.bfloat16)
        return largest

    def mix(u, i, largest):
        rows = slice(i * TILE, (i + 1) * TILE)
        sums = jnp.dot(p_ref[u, rows, :], val_ref[u], preferred_element_type=jnp.float32)
        finish(u, rows, sums, largest)

    blocks = [(u, i) for i in range(tiles) for u in range(heads)]
    score(*blocks[0])
    waiting = None
    for at, block in enumerate(blocks):
        if at + 1 < len(blocks):
            score(*blocks[at + 1])
        largest = weigh(*block)
        if waiting is not None:
            mix(*waiting)
        waiting = (*block, largest)
    mix(*waiting)


def bias_of(meta_ref, at, tiles):
    return [jnp.where(meta_ref[at + j] == 0, OUT_OF_WINDOW, 0.0) for j in range(tiles)]


def head_cols(u):
    return slice(u * HEAD_DIM, (u + 1) * HEAD_DIM)


def ones_once(val_ref):
    @pl.when(pl.program_id(0) == 0)
    def _():
        for u in range(val_ref.shape[0]):
            val_ref[u, :, HEAD_DIM:] = jnp.ones(val_ref.shape[1:2] + (HEAD_DIM,), jnp.bfloat16)


def own_kernel(meta_ref, q_ref, k_ref, v_ref, *rest):
    o_ref, val_ref, s_ref, p_ref = rest[-4:]
    tiles = k_ref.shape[0] // TILE
    heads = val_ref.shape[0]
    ones_once(val_ref)
    for u in range(heads):
        val_ref[u, :, :HEAD_DIM] = v_ref[:, head_cols(u)]

    def finish(u, rows, sums, largest):
        weight = sums[:, HEAD_DIM:]
        o_ref[rows, head_cols(2 * u)] = sums[:, :HEAD_DIM] / weight
        o_ref[rows, head_cols(2 * u + 1)] = largest + jnp.log2(weight)

    attend_blocks(
        heads,
        tiles,
        lambda u, rows: q_ref[rows, head_cols(u)],
        lambda u: k_ref[:, head_cols(u)],
        [bias_of(meta_ref, i * tiles, tiles) for i in range(tiles)],
        val_ref,
        s_ref,
        p_ref,
        lambda u, rows: None,
        finish,
    )


def attend_own(flags, q_hat, k_hat, values, first, heads, out=None):
    rows, width = q_hat.shape
    step = 1 if heads % 2 or first % 2 else 2
    wide = step * HEAD_DIM
    column = pl.BlockSpec((rows, wide), lambda h, flags: (0, first // step + h))
    operands, in_specs, aliases = [q_hat, k_hat, values], [column] * 3, {}
    if out is not None:
        in_specs.append(pl.BlockSpec(memory_space=pl.ANY))
        operands.append(out)
        aliases = {len(operands): 0}
    return pl.pallas_call(
        own_kernel,
        grid_spec=pltpu.PrefetchScalarGridSpec(
            num_scalar_prefetch=1,
            grid=(heads // step,),
            in_specs=in_specs,
            out_specs=pl.BlockSpec((rows, 2 * wide), lambda h, flags: (0, first // step + h)),
            scratch_shapes=[
                pltpu.VMEM((step, rows, 2 * HEAD_DIM), jnp.bfloat16),
                pltpu.VMEM((step, rows, rows), jnp.float32),
                pltpu.VMEM((step, rows, rows), jnp.bfloat16),
            ],
        ),
        out_shape=jax.ShapeDtypeStruct((rows, 2 * width), jnp.float32),
        input_output_aliases=aliases,
        compiler_params=pltpu.CompilerParams(vmem_limit_bytes=40 * 2**20),
        cost_estimate=cost(heads, rows, rows),
    )(flags, *operands)


def rest_kernel(shards, meta_ref, q_ref, part_ref, kn_ref, vn_ref, *rest):
    text_refs = rest[:shards]
    o_ref, key_ref, val_ref, s_ref, p_ref = rest[-5:]
    near = kn_ref.shape[0]
    heads = val_ref.shape[0]
    ones_once(val_ref)
    for u in range(heads):
        cols = head_cols(u)
        key_ref[u, :near, :] = kn_ref[:, cols]
        val_ref[u, :near, :HEAD_DIM] = vn_ref[:, cols]
        at = near
        for text_ref in text_refs:
            rows = slice(at, at + text_ref.shape[1])
            key_ref[u, rows, :] = text_ref[0, :, cols]
            val_ref[u, rows, :HEAD_DIM] = text_ref[1, :, cols]
            at += text_ref.shape[1]

    def floor_of(u, rows):
        return part_ref[rows, head_cols(2 * u + 1)]

    def finish(u, rows, sums, largest):
        kept = jnp.exp2(floor_of(u, rows) - largest)
        summed = sums[:, :HEAD_DIM] + kept * part_ref[rows, head_cols(2 * u)]
        o_ref[rows, head_cols(u)] = (summed / (sums[:, HEAD_DIM:] + kept)).astype(jnp.bfloat16)

    near_tiles = near // TILE
    attend_blocks(
        heads,
        FRAME_TILES,
        lambda u, rows: q_ref[rows, head_cols(u)],
        lambda u: key_ref[u],
        [bias_of(meta_ref, 2 + i * near_tiles, near_tiles) for i in range(FRAME_TILES)],
        val_ref,
        s_ref,
        p_ref,
        floor_of,
        finish,
    )


def attend_rest(meta, q_hat, part, near_k, near_v, shards, first, heads, out=None):
    rows, width = q_hat.shape
    total = FRAME + TXT
    step = 1 if heads % 2 or first % 2 else 2
    wide = step * HEAD_DIM
    frame_block = pl.BlockSpec((FRAME, wide), lambda h, meta: (meta[0], first // step + h))
    in_specs = [
        frame_block,
        pl.BlockSpec((FRAME, 2 * wide), lambda h, meta: (meta[0], first // step + h)),
        pl.BlockSpec((None, FRAME, wide), lambda h, meta: (0, 0, h)),
        pl.BlockSpec((None, FRAME, wide), lambda h, meta: (near_v.shape[0] - 1, 0, h)),
    ] + [
        pl.BlockSpec(
            (2, None, shard.shape[2], wide), lambda h, meta: (0, meta[1], 0, first // step + h)
        )
        for shard in shards
    ]
    operands = [q_hat, part, near_k, near_v, *shards]
    aliases = {}
    if out is not None:
        in_specs.append(pl.BlockSpec(memory_space=pl.ANY))
        operands.append(out)
        aliases = {len(operands): 0}
    return pl.pallas_call(
        functools.partial(rest_kernel, len(shards)),
        grid_spec=pltpu.PrefetchScalarGridSpec(
            num_scalar_prefetch=1,
            grid=(heads // step,),
            in_specs=in_specs,
            out_specs=frame_block,
            scratch_shapes=[
                pltpu.VMEM((step, total, HEAD_DIM), jnp.bfloat16),
                pltpu.VMEM((step, total, 2 * HEAD_DIM), jnp.bfloat16),
                pltpu.VMEM((step, FRAME, total), jnp.float32),
                pltpu.VMEM((step, FRAME, total), jnp.bfloat16),
            ],
        ),
        out_shape=jax.ShapeDtypeStruct((rows, width), jnp.bfloat16),
        input_output_aliases=aliases,
        compiler_params=pltpu.CompilerParams(vmem_limit_bytes=32 * 2**20),
        cost_estimate=cost(heads, FRAME, total),
    )(meta, *operands)


def side_route(count, level):
    last = count // 2 - 1
    first, second, is_straight = [], [], [False] * count
    for k in range(last):
        low, high = 2 * k + 1, 2 * k + 2
        for source, target, relays in ((low, high, k < level), (high, low, k >= last - level)):
            if relays:
                first.append((source, source ^ 1))
                second.append((source ^ 1, target))
            else:
                first.append((source, target))
                is_straight[target] = True
    return first, second, is_straight


def after(value, *others):
    return lax.optimization_barrier((value, *others))[0]


def local(
    queries, keys, values, query_gain, key_gain, shapes, windows, text_keys, text_values, owner
):
    rows, width = queries.shape
    heads = width // HEAD_DIM
    count = lax.axis_size("seq")
    me = lax.axis_index("seq")
    odd = me % 2
    pair = [(i, i ^ 1) for i in range(count)]
    pair_frame, side_frame = 1 - odd, odd

    chosen = choose(owner, text_keys, text_values)
    both = jnp.concatenate([chosen, lax.ppermute(chosen, "seq", pair)], axis=2)
    pair_values = lax.dynamic_slice_in_dim(after(values, chosen), pair_frame * FRAME, FRAME, 0)
    near_values = lax.ppermute(pair_values[None], "seq", pair)
    if count <= 8:
        shards = [both] + [
            lax.ppermute(both, "seq", [(i, (i + 2 * k) % count) for i in range(count)])
            for k in range(1, count // 2)
        ]
    else:
        groups = [list(range(start, count, 2)) for start in range(2)]
        shards = [lax.all_gather(both, "seq", axis=2, tiled=True, axis_index_groups=groups)]

    place, own_flags, pair_meta, side_meta = plan(me, shapes, windows)
    query_wide, key_wide, _ = lax.optimization_barrier((queries, keys, chosen))
    query_wide = query_wide.astype(jnp.float32)
    key_wide = key_wide.astype(jnp.float32)
    squares = head_sum(
        jnp.stack([jnp.sum(query_wide * query_wide, axis=1), jnp.sum(key_wide * key_wide, axis=1)])
    )
    q_hat, k_hat = turn(place, squares, queries, keys, query_gain, key_gain)
    pair_keys = lax.dynamic_slice_in_dim(k_hat, pair_frame * FRAME, FRAME, 0)[None]
    near_keys = lax.ppermute(pair_keys, "seq", pair)
    part = attend_own(own_flags, q_hat, k_hat, values, 0, heads)
    out = attend_rest(pair_meta, q_hat, part, near_keys, near_values, shards, 0, heads)

    few = max(1, heads * 2 // 5)
    relays = count // 2 - 1 if count == 8 else 0
    parcels = (
        (few, relays, (near_values,)),
        (heads - few, 0, (near_keys, part, *shards)),
    )
    side_keys = lax.dynamic_slice_in_dim(k_hat, side_frame * FRAME, FRAME, 0)
    side_values = lax.dynamic_slice_in_dim(values, side_frame * FRAME, FRAME, 0)
    side_parcels = []
    start = 0
    for step, level, gate in parcels:
        cols = slice(start * HEAD_DIM, (start + step) * HEAD_DIM)
        parcel = jnp.stack([side_keys[:, cols], side_values[:, cols]])
        straight, relayed, is_straight = side_route(count, level)
        arrived = lax.ppermute(after(parcel, *gate), "seq", straight)
        if relayed:
            forwarded = lax.ppermute(arrived, "seq", relayed)
            if any(is_straight):
                forwarded = jnp.where(jnp.asarray(is_straight)[me], arrived, forwarded)
            arrived = forwarded
        side_parcels.append(arrived)
        start += step
    start = 0
    for (step, *_), parcel in zip(parcels, side_parcels):
        out = attend_rest(side_meta, q_hat, part, parcel, parcel, shards, start, step, out)
        start += step
    return out


def solution(mesh):
    placed = (
        P("seq", "head"),
        P("seq", "head"),
        P("seq", "head"),
        P("head"),
        P("head"),
        P(),
        P("seq", None),
        P(None, "seq", "head"),
        P(None, "seq", "head"),
        P(),
    )
    return jax.shard_map(
        local, mesh=mesh, in_specs=placed, out_specs=P("seq", "head"), check_vma=False
    )
```

```python
import functools
import math

import jax
import jax.numpy as jnp
import numpy as np
from jax import lax
from jax.experimental import pallas as pl
from jax.experimental.pallas import tpu as pltpu
from jax.sharding import PartitionSpec as P

HEAD_DIM = 128
D = 5120
TILE_H = 8
TILE_W = 16
TILE = 128
FRAME_TILES = 4
FRAME = FRAME_TILES * TILE
TXT = 256
WIN = 27
EPSILON = 1e-06
OUT_OF_WINDOW = -1e30
SMALL = pl.CostEstimate(flops=1000, bytes_accessed=1000, transcendentals=0)


def cost(heads, rows, keys):
    return pl.CostEstimate(
        flops=8 * heads * rows * keys * HEAD_DIM,
        bytes_accessed=6 * heads * rows * keys,
        transcendentals=heads * rows * keys,
    )


def lane_tables():
    third = HEAD_DIM // 6
    part_sizes = (HEAD_DIM - 4 * third, 2 * third, 2 * third)
    part = np.concatenate([np.full(size, at) for at, size in enumerate(part_sizes)])
    pair_at = np.concatenate([np.arange(size) // 2 * 2 for size in part_sizes])
    size_at = np.concatenate([np.full(size, size) for size in part_sizes])
    frequency = 10000.0 ** (-jnp.asarray(pair_at, jnp.float32) / jnp.asarray(size_at, jnp.float32))
    return jnp.asarray(part, jnp.int32)[None, :], frequency[None, :]


def plan_kernel(samples, me_ref, shapes_ref, windows_ref, place_ref, own_ref, pair_ref, side_ref):
    me = me_ref[0]
    tiles = 2 * FRAME_TILES
    first = me * tiles
    odd = lax.rem(me, 2)
    narrow = []
    for f in range(2):
        frame_at = first + f * FRAME_TILES
        start, own_start, sample = 0, 0, 0
        single = shapes_ref[2] == TILE_W
        for s in range(samples):
            if s:
                inside = frame_at >= start
                sample = jnp.where(inside, s, sample)
                own_start = jnp.where(inside, start, own_start)
                single = jnp.where(inside, shapes_ref[3 * s + 2] == TILE_W, single)
            start = start + FRAME_TILES * shapes_ref[3 * s]
        narrow.append(single)
        moment = (frame_at - own_start) // FRAME_TILES
        for a in range(FRAME_TILES):
            at = 3 * (f * FRAME_TILES + a)
            place_ref[at] = moment
            place_ref[at + 1] = jnp.where(single, a, a // 2)
            place_ref[at + 2] = jnp.where(single, 0, a % 2)
        is_pair = odd == 1 - f
        for ref, wanted in ((pair_ref, is_pair), (side_ref, jnp.logical_not(is_pair))):

            @pl.when(wanted)
            def _(ref=ref, f=f, sample=sample):
                ref[0] = f
                ref[1] = sample

    def flag(f, a, step, b):
        tall = (step + 1) * 9 + (b - a + 1) * 3 + 1
        square = (step + 1) * 9 + (b // 2 - a // 2 + 1) * 3 + b % 2 - a % 2 + 1
        row = (f * FRAME_TILES + a) * WIN
        key = first + (f + step) * FRAME_TILES + b
        if abs(b - a) > 1:
            found = jnp.logical_and(jnp.logical_not(narrow[f]), windows_ref[row + square] == key)
        else:
            found = windows_ref[row + jnp.where(narrow[f], tall, square)] == key
        return jnp.logical_and(found, key >= 0).astype(jnp.int32)

    for f in range(2):
        near_step = 2 * f - 1
        near = [flag(f, a, near_step, b) for a in range(FRAME_TILES) for b in range(FRAME_TILES)]
        is_pair = odd == 1 - f
        for ref, wanted in ((pair_ref, is_pair), (side_ref, jnp.logical_not(is_pair))):

            @pl.when(wanted)
            def _(ref=ref, near=near):
                for at, value in enumerate(near):
                    ref[2 + at] = value

        for a in range(FRAME_TILES):
            for g in range(2):
                for b in range(FRAME_TILES):
                    at = (f * FRAME_TILES + a) * tiles + g * FRAME_TILES + b
                    own_ref[at] = flag(f, a, g - f, b)


def plan(me, shapes, windows):
    samples = shapes.shape[0]
    tiles = 2 * FRAME_TILES
    smem = pl.BlockSpec(memory_space=pltpu.SMEM)
    sizes = (3 * tiles, tiles * tiles, 2 + FRAME_TILES**2, 2 + FRAME_TILES**2)
    return pl.pallas_call(
        functools.partial(plan_kernel, samples),
        in_specs=[smem] * 3,
        out_specs=[smem] * 4,
        out_shape=[jax.ShapeDtypeStruct((size,), jnp.int32) for size in sizes],
        cost_estimate=SMALL,
    )(me.reshape(1), shapes.reshape(-1), windows.reshape(-1))


def head_sum(partial):
    count = lax.axis_size("head")
    if count & (count - 1):
        return lax.psum(partial, "head")
    step = 1
    while step < count:
        partial = partial + lax.ppermute(partial, "head", [(i, i ^ step) for i in range(count)])
        step *= 2
    return partial


def exchange_pairs(row):
    lane = lax.broadcasted_iota(jnp.int32, row.shape, 1)
    return jnp.where(lane % 2 == 0, pltpu.roll(row, HEAD_DIM - 1, 1), pltpu.roll(row, 1, 1))


def turn_kernel(place_ref, part_ref, frequency_ref, squares_ref, *refs):
    fields, gains, outs, tables = refs[:2], refs[2:4], refs[4:6], refs[6:]
    rows, width = fields[0].shape

    @pl.when(pl.program_id(0) == 0)
    def _():
        token = lax.broadcasted_iota(jnp.int32, (TILE, HEAD_DIM), 0)
        lane = lax.broadcasted_iota(jnp.int32, (TILE, HEAD_DIM), 1)
        part = part_ref[...]
        for i in range(rows // TILE):
            time_pos, band, column = (place_ref[3 * i + axis] for axis in range(3))
            row_pos = band * TILE_H + token // TILE_W
            col_pos = column * TILE_W + token % TILE_W
            position = jnp.where(part == 0, time_pos, jnp.where(part == 1, row_pos, col_pos))
            angles = position.astype(jnp.float32) * frequency_ref[...]
            cosine = jnp.cos(angles)
            sine = jnp.sin(angles) * jnp.where(lane % 2 == 0, -1.0, 1.0)
            at = slice(i * TILE, (i + 1) * TILE)
            for n, factor in enumerate((HEAD_DIM**-0.5 * math.log2(math.e), 1.0)):
                scale = lax.rsqrt(squares_ref[n : n + 1, at] / D + EPSILON) * factor
                scale = jnp.transpose(jnp.broadcast_to(scale, (TILE, HEAD_DIM)))
                tables[2 * n][at, :] = cosine * scale
                tables[2 * n + 1][at, :] = sine * scale

    row = lax.broadcasted_iota(jnp.int32, (HEAD_DIM, HEAD_DIM), 0)
    col = lax.broadcasted_iota(jnp.int32, (HEAD_DIM, HEAD_DIM), 1)
    exchange = (row == col + 1 - 2 * (col % 2)).astype(jnp.bfloat16)
    for n in range(2):
        for u in range(width // HEAD_DIM):
            cols = slice(u * HEAD_DIM, (u + 1) * HEAD_DIM)
            x = fields[n][:, cols]
            gain = jnp.broadcast_to(gains[n][:, cols], (8, HEAD_DIM))
            swapped = jnp.dot(x, exchange, preferred_element_type=jnp.float32)
            turned = (x.astype(jnp.float32) * gain[:1]) * tables[2 * n][...]
            turned += (swapped * exchange_pairs(gain)[:1]) * tables[2 * n + 1][...]
            outs[n][:, cols] = turned.astype(jnp.bfloat16)


def turn(place, squares, queries, keys, query_gain, key_gain):
    rows, width = queries.shape
    heads = width // HEAD_DIM
    step = 2 - heads % 2
    part, frequency = lane_tables()
    column = pl.BlockSpec((rows, step * HEAD_DIM), lambda h, place: (0, h))
    line = pl.BlockSpec((1, step * HEAD_DIM), lambda h, place: (0, h))
    lanes = pl.BlockSpec((1, HEAD_DIM), lambda h, place: (0, 0))
    whole = pl.BlockSpec((2, rows), lambda h, place: (0, 0))
    return pl.pallas_call(
        turn_kernel,
        grid_spec=pltpu.PrefetchScalarGridSpec(
            num_scalar_prefetch=1,
            grid=(heads // step,),
            in_specs=[lanes, lanes, whole, column, column, line, line],
            out_specs=[column, column],
            scratch_shapes=[pltpu.VMEM((rows, HEAD_DIM), jnp.float32) for _ in range(4)],
        ),
        out_shape=[jax.ShapeDtypeStruct((rows, width), jnp.bfloat16)] * 2,
        compiler_params=pltpu.CompilerParams(vmem_limit_bytes=24 * 2**20),
        cost_estimate=SMALL,
    )(
        place,
        part,
        frequency,
        squares,
        queries,
        keys,
        query_gain.reshape(1, width),
        key_gain.reshape(1, width),
    )


def choose_kernel(owner_ref, keys_ref, values_ref, o_ref):
    o_ref[0] = keys_ref[...]
    o_ref[1] = values_ref[...]


def choose(owner, text_keys, text_values):
    panels, rows, width = text_keys.shape
    samples = owner.shape[0]
    panel = pl.BlockSpec((None, rows, width), lambda s, owner: (owner[s], 0, 0))
    return pl.pallas_call(
        choose_kernel,
        grid_spec=pltpu.PrefetchScalarGridSpec(
            num_scalar_prefetch=1,
            grid=(samples,),
            in_specs=[panel, panel],
            out_specs=pl.BlockSpec((2, None, rows, width), lambda s, owner: (0, s, 0, 0)),
        ),
        out_shape=jax.ShapeDtypeStruct((2, samples, rows, width), text_keys.dtype),
        cost_estimate=SMALL,
    )(owner, text_keys, text_values)


def attend_blocks(heads, tiles, query, keys, bias, val_ref, s_ref, p_ref, floor_of, finish):
    def score(u, i):
        rows = slice(i * TILE, (i + 1) * TILE)
        s_ref[u, rows, :] = lax.dot_general(
            query(u, rows),
            keys(u),
            (((1,), (1,)), ((), ())),
            preferred_element_type=jnp.float32,
        )

    def weigh(u, i):
        rows = slice(i * TILE, (i + 1) * TILE)
        largest = None
        for j in range(s_ref.shape[2] // TILE):
            part = s_ref[u, rows, j * TILE : (j + 1) * TILE]
            if j < len(bias[i]):
                part = part + bias[i][j]
            largest = part if largest is None else jnp.maximum(largest, part)
        largest = jnp.max(largest, axis=1, keepdims=True)
        floor = floor_of(u, rows)
        if floor is None:
            largest = jnp.broadcast_to(largest, (TILE, HEAD_DIM))
        else:
            largest = jnp.maximum(largest, floor)
        for j in range(s_ref.shape[2] // TILE):
            cols = slice(j * TILE, (j + 1) * TILE)
            top = largest - bias[i][j] if j < len(bias[i]) else largest
            p_ref[u, rows, cols] = jnp.exp2(s_ref[u, rows, cols] - top).astype(jnp.bfloat16)
        return largest

    def mix(u, i, largest):
        rows = slice(i * TILE, (i + 1) * TILE)
        sums = jnp.dot(p_ref[u, rows, :], val_ref[u], preferred_element_type=jnp.float32)
        finish(u, rows, sums, largest)

    blocks = [(u, i) for i in range(tiles) for u in range(heads)]
    score(*blocks[0])
    score(*blocks[1])
    waiting = None
    for at, block in enumerate(blocks):
        if at + 2 < len(blocks):
            score(*blocks[at + 2])
        largest = weigh(*block)
        if waiting is not None:
            mix(*waiting)
        waiting = (*block, largest)
    mix(*waiting)


def bias_of(meta_ref, at, tiles):
    return [jnp.where(meta_ref[at + j] == 0, OUT_OF_WINDOW, 0.0) for j in range(tiles)]


def head_cols(u):
    return slice(u * HEAD_DIM, (u + 1) * HEAD_DIM)


def ones_once(val_ref):
    @pl.when(pl.program_id(0) == 0)
    def _():
        for u in range(val_ref.shape[0]):
            val_ref[u, :, HEAD_DIM:] = jnp.ones(val_ref.shape[1:2] + (HEAD_DIM,), jnp.bfloat16)


def own_kernel(meta_ref, q_ref, k_ref, v_ref, *rest):
    o_ref, val_ref, s_ref, p_ref = rest[-4:]
    tiles = k_ref.shape[0] // TILE
    heads = val_ref.shape[0]
    ones_once(val_ref)
    for u in range(heads):
        val_ref[u, :, :HEAD_DIM] = v_ref[:, head_cols(u)]

    def finish(u, rows, sums, largest):
        weight = sums[:, HEAD_DIM:]
        o_ref[rows, head_cols(2 * u)] = sums[:, :HEAD_DIM] / weight
        o_ref[rows, head_cols(2 * u + 1)] = largest + jnp.log2(weight)

    attend_blocks(
        heads,
        tiles,
        lambda u, rows: q_ref[rows, head_cols(u)],
        lambda u: k_ref[:, head_cols(u)],
        [bias_of(meta_ref, i * tiles, tiles) for i in range(tiles)],
        val_ref,
        s_ref,
        p_ref,
        lambda u, rows: None,
        finish,
    )


def attend_own(flags, q_hat, k_hat, values, first, heads, out=None):
    rows, width = q_hat.shape
    step = 1 if heads % 2 or first % 2 else 2
    wide = step * HEAD_DIM
    column = pl.BlockSpec((rows, wide), lambda h, flags: (0, first // step + h))
    operands, in_specs, aliases = [q_hat, k_hat, values], [column] * 3, {}
    if out is not None:
        in_specs.append(pl.BlockSpec(memory_space=pl.ANY))
        operands.append(out)
        aliases = {len(operands): 0}
    return pl.pallas_call(
        own_kernel,
        grid_spec=pltpu.PrefetchScalarGridSpec(
            num_scalar_prefetch=1,
            grid=(heads // step,),
            in_specs=in_specs,
            out_specs=pl.BlockSpec((rows, 2 * wide), lambda h, flags: (0, first // step + h)),
            scratch_shapes=[
                pltpu.VMEM((step, rows, 2 * HEAD_DIM), jnp.bfloat16),
                pltpu.VMEM((step, rows, rows), jnp.float32),
                pltpu.VMEM((step, rows, rows), jnp.bfloat16),
            ],
        ),
        out_shape=jax.ShapeDtypeStruct((rows, 2 * width), jnp.float32),
        input_output_aliases=aliases,
        compiler_params=pltpu.CompilerParams(vmem_limit_bytes=40 * 2**20),
        cost_estimate=cost(heads, rows, rows),
    )(flags, *operands)


def rest_kernel(shards, meta_ref, q_ref, part_ref, kn_ref, vn_ref, *rest):
    text_refs = rest[:shards]
    o_ref, key_ref, val_ref, s_ref, p_ref = rest[-5:]
    near = kn_ref.shape[0]
    heads = val_ref.shape[0]
    ones_once(val_ref)
    for u in range(heads):
        cols = head_cols(u)
        key_ref[u, :near, :] = kn_ref[:, cols]
        val_ref[u, :near, :HEAD_DIM] = vn_ref[:, cols]
        at = near
        for text_ref in text_refs:
            rows = slice(at, at + text_ref.shape[1])
            key_ref[u, rows, :] = text_ref[0, :, cols]
            val_ref[u, rows, :HEAD_DIM] = text_ref[1, :, cols]
            at += text_ref.shape[1]

    def floor_of(u, rows):
        return part_ref[rows, head_cols(2 * u + 1)]

    def finish(u, rows, sums, largest):
        kept = jnp.exp2(floor_of(u, rows) - largest)
        summed = sums[:, :HEAD_DIM] + kept * part_ref[rows, head_cols(2 * u)]
        o_ref[rows, head_cols(u)] = (summed / (sums[:, HEAD_DIM:] + kept)).astype(jnp.bfloat16)

    near_tiles = near // TILE
    attend_blocks(
        heads,
        FRAME_TILES,
        lambda u, rows: q_ref[rows, head_cols(u)],
        lambda u: key_ref[u],
        [bias_of(meta_ref, 2 + i * near_tiles, near_tiles) for i in range(FRAME_TILES)],
        val_ref,
        s_ref,
        p_ref,
        floor_of,
        finish,
    )


def attend_rest(meta, q_hat, part, near_k, near_v, shards, first, heads, out=None):
    rows, width = q_hat.shape
    total = FRAME + TXT
    step = 1 if heads % 2 or first % 2 else 2
    wide = step * HEAD_DIM
    frame_block = pl.BlockSpec((FRAME, wide), lambda h, meta: (meta[0], first // step + h))
    in_specs = [
        frame_block,
        pl.BlockSpec((FRAME, 2 * wide), lambda h, meta: (meta[0], first // step + h)),
        pl.BlockSpec((None, FRAME, wide), lambda h, meta: (0, 0, h)),
        pl.BlockSpec((None, FRAME, wide), lambda h, meta: (near_v.shape[0] - 1, 0, h)),
    ] + [
        pl.BlockSpec(
            (2, None, shard.shape[2], wide), lambda h, meta: (0, meta[1], 0, first // step + h)
        )
        for shard in shards
    ]
    operands = [q_hat, part, near_k, near_v, *shards]
    aliases = {}
    if out is not None:
        in_specs.append(pl.BlockSpec(memory_space=pl.ANY))
        operands.append(out)
        aliases = {len(operands): 0}
    return pl.pallas_call(
        functools.partial(rest_kernel, len(shards)),
        grid_spec=pltpu.PrefetchScalarGridSpec(
            num_scalar_prefetch=1,
            grid=(heads // step,),
            in_specs=in_specs,
            out_specs=frame_block,
            scratch_shapes=[
                pltpu.VMEM((step, total, HEAD_DIM), jnp.bfloat16),
                pltpu.VMEM((step, total, 2 * HEAD_DIM), jnp.bfloat16),
                pltpu.VMEM((step, FRAME, total), jnp.float32),
                pltpu.VMEM((step, FRAME, total), jnp.bfloat16),
            ],
        ),
        out_shape=jax.ShapeDtypeStruct((rows, width), jnp.bfloat16),
        input_output_aliases=aliases,
        compiler_params=pltpu.CompilerParams(vmem_limit_bytes=32 * 2**20),
        cost_estimate=cost(heads, FRAME, total),
    )(meta, *operands)


def side_route(count, level):
    last = count // 2 - 1
    first, second, is_straight = [], [], [False] * count
    for k in range(last):
        low, high = 2 * k + 1, 2 * k + 2
        for source, target, relays in ((low, high, k < level), (high, low, k >= last - level)):
            if relays:
                first.append((source, source ^ 1))
                second.append((source ^ 1, target))
            else:
                first.append((source, target))
                is_straight[target] = True
    return first, second, is_straight


def after(value, *others):
    return lax.optimization_barrier((value, *others))[0]


def local(
    queries, keys, values, query_gain, key_gain, shapes, windows, text_keys, text_values, owner
):
    rows, width = queries.shape
    heads = width // HEAD_DIM
    count = lax.axis_size("seq")
    me = lax.axis_index("seq")
    odd = me % 2
    pair = [(i, i ^ 1) for i in range(count)]
    pair_frame, side_frame = 1 - odd, odd

    chosen = choose(owner, text_keys, text_values)
    both = jnp.concatenate([chosen, lax.ppermute(chosen, "seq", pair)], axis=2)
    pair_values = lax.dynamic_slice_in_dim(after(values, chosen), pair_frame * FRAME, FRAME, 0)
    near_values = lax.ppermute(pair_values[None], "seq", pair)
    if count <= 8:
        shards = [both] + [
            lax.ppermute(both, "seq", [(i, (i + 2 * k) % count) for i in range(count)])
            for k in range(1, count // 2)
        ]
    else:
        groups = [list(range(start, count, 2)) for start in range(2)]
        shards = [lax.all_gather(both, "seq", axis=2, tiled=True, axis_index_groups=groups)]

    place, own_flags, pair_meta, side_meta = plan(me, shapes, windows)
    query_wide, key_wide, _ = lax.optimization_barrier((queries, keys, chosen))
    query_wide = query_wide.astype(jnp.float32)
    key_wide = key_wide.astype(jnp.float32)
    squares = head_sum(
        jnp.stack([jnp.sum(query_wide * query_wide, axis=1), jnp.sum(key_wide * key_wide, axis=1)])
    )
    q_hat, k_hat = turn(place, squares, queries, keys, query_gain, key_gain)
    pair_keys = lax.dynamic_slice_in_dim(k_hat, pair_frame * FRAME, FRAME, 0)[None]
    near_keys = lax.ppermute(pair_keys, "seq", pair)
    part = attend_own(own_flags, q_hat, k_hat, values, 0, heads)
    out = attend_rest(pair_meta, q_hat, part, near_keys, near_values, shards, 0, heads)

    few = max(1, heads * 2 // 5)
    relays = count // 2 - 1 if count == 8 else 0
    parcels = (
        (few, relays, (near_values,)),
        (heads - few, 0, (near_keys, part, *shards)),
    )
    side_keys = lax.dynamic_slice_in_dim(k_hat, side_frame * FRAME, FRAME, 0)
    side_values = lax.dynamic_slice_in_dim(values, side_frame * FRAME, FRAME, 0)
    side_parcels = []
    start = 0
    for step, level, gate in parcels:
        cols = slice(start * HEAD_DIM, (start + step) * HEAD_DIM)
        parcel = jnp.stack([side_keys[:, cols], side_values[:, cols]])
        straight, relayed, is_straight = side_route(count, level)
        arrived = lax.ppermute(after(parcel, *gate), "seq", straight)
        if relayed:
            forwarded = lax.ppermute(arrived, "seq", relayed)
            if any(is_straight):
                forwarded = jnp.where(jnp.asarray(is_straight)[me], arrived, forwarded)
            arrived = forwarded
        side_parcels.append(arrived)
        start += step
    start = 0
    for (step, *_), parcel in zip(parcels, side_parcels):
        out = attend_rest(side_meta, q_hat, part, parcel, parcel, shards, start, step, out)
        start += step
    return out


def solution(mesh):
    placed = (
        P("seq", "head"),
        P("seq", "head"),
        P("seq", "head"),
        P("head"),
        P("head"),
        P(),
        P("seq", None),
        P(None, "seq", "head"),
        P(None, "seq", "head"),
        P(),
    )
    return jax.shard_map(
        local, mesh=mesh, in_specs=placed, out_specs=P("seq", "head"), check_vma=False
    )
```

```python
import functools
import math

import jax
import jax.numpy as jnp
import numpy as np
from jax import lax
from jax.experimental import pallas as pl
from jax.experimental.pallas import tpu as pltpu
from jax.sharding import PartitionSpec as P

HEAD_DIM = 128
D = 5120
TILE_H = 8
TILE_W = 16
TILE = 128
FRAME_TILES = 4
FRAME = FRAME_TILES * TILE
TXT = 256
WIN = 27
EPSILON = 1e-06
OUT_OF_WINDOW = -1e30
SMALL = pl.CostEstimate(flops=1000, bytes_accessed=1000, transcendentals=0)


def cost(heads, rows, keys):
    return pl.CostEstimate(
        flops=8 * heads * rows * keys * HEAD_DIM,
        bytes_accessed=6 * heads * rows * keys,
        transcendentals=heads * rows * keys,
    )


def lane_tables():
    third = HEAD_DIM // 6
    part_sizes = (HEAD_DIM - 4 * third, 2 * third, 2 * third)
    part = np.concatenate([np.full(size, at) for at, size in enumerate(part_sizes)])
    pair_at = np.concatenate([np.arange(size) // 2 * 2 for size in part_sizes])
    size_at = np.concatenate([np.full(size, size) for size in part_sizes])
    frequency = 10000.0 ** (-jnp.asarray(pair_at, jnp.float32) / jnp.asarray(size_at, jnp.float32))
    return jnp.asarray(part, jnp.int32)[None, :], frequency[None, :]


def plan_kernel(samples, me_ref, shapes_ref, windows_ref, place_ref, own_ref, pair_ref, side_ref):
    me = me_ref[0]
    tiles = 2 * FRAME_TILES
    first = me * tiles
    odd = lax.rem(me, 2)
    narrow = []
    for f in range(2):
        frame_at = first + f * FRAME_TILES
        start, own_start, sample = 0, 0, 0
        single = shapes_ref[2] == TILE_W
        for s in range(samples):
            if s:
                inside = frame_at >= start
                sample = jnp.where(inside, s, sample)
                own_start = jnp.where(inside, start, own_start)
                single = jnp.where(inside, shapes_ref[3 * s + 2] == TILE_W, single)
            start = start + FRAME_TILES * shapes_ref[3 * s]
        narrow.append(single)
        moment = (frame_at - own_start) // FRAME_TILES
        for a in range(FRAME_TILES):
            at = 3 * (f * FRAME_TILES + a)
            place_ref[at] = moment
            place_ref[at + 1] = jnp.where(single, a, a // 2)
            place_ref[at + 2] = jnp.where(single, 0, a % 2)
        is_pair = odd == 1 - f
        for ref, wanted in ((pair_ref, is_pair), (side_ref, jnp.logical_not(is_pair))):

            @pl.when(wanted)
            def _(ref=ref, f=f, sample=sample):
                ref[0] = f
                ref[1] = sample

    def flag(f, a, step, b):
        tall = (step + 1) * 9 + (b - a + 1) * 3 + 1
        square = (step + 1) * 9 + (b // 2 - a // 2 + 1) * 3 + b % 2 - a % 2 + 1
        row = (f * FRAME_TILES + a) * WIN
        key = first + (f + step) * FRAME_TILES + b
        if abs(b - a) > 1:
            found = jnp.logical_and(jnp.logical_not(narrow[f]), windows_ref[row + square] == key)
        else:
            found = windows_ref[row + jnp.where(narrow[f], tall, square)] == key
        return jnp.logical_and(found, key >= 0).astype(jnp.int32)

    for f in range(2):
        near_step = 2 * f - 1
        near = [flag(f, a, near_step, b) for a in range(FRAME_TILES) for b in range(FRAME_TILES)]
        is_pair = odd == 1 - f
        for ref, wanted in ((pair_ref, is_pair), (side_ref, jnp.logical_not(is_pair))):

            @pl.when(wanted)
            def _(ref=ref, near=near):
                for at, value in enumerate(near):
                    ref[2 + at] = value

        for a in range(FRAME_TILES):
            for g in range(2):
                for b in range(FRAME_TILES):
                    at = (f * FRAME_TILES + a) * tiles + g * FRAME_TILES + b
                    own_ref[at] = flag(f, a, g - f, b)


def plan(me, shapes, windows):
    samples = shapes.shape[0]
    tiles = 2 * FRAME_TILES
    smem = pl.BlockSpec(memory_space=pltpu.SMEM)
    sizes = (3 * tiles, tiles * tiles, 2 + FRAME_TILES**2, 2 + FRAME_TILES**2)
    return pl.pallas_call(
        functools.partial(plan_kernel, samples),
        in_specs=[smem] * 3,
        out_specs=[smem] * 4,
        out_shape=[jax.ShapeDtypeStruct((size,), jnp.int32) for size in sizes],
        cost_estimate=SMALL,
    )(me.reshape(1), shapes.reshape(-1), windows.reshape(-1))


def head_sum(partial):
    count = lax.axis_size("head")
    if count & (count - 1):
        return lax.psum(partial, "head")
    step = 1
    while step < count:
        partial = partial + lax.ppermute(partial, "head", [(i, i ^ step) for i in range(count)])
        step *= 2
    return partial


def exchange_pairs(row):
    lane = lax.broadcasted_iota(jnp.int32, row.shape, 1)
    return jnp.where(lane % 2 == 0, pltpu.roll(row, HEAD_DIM - 1, 1), pltpu.roll(row, 1, 1))


def turn_kernel(place_ref, part_ref, frequency_ref, squares_ref, *refs):
    fields, gains, outs, tables = refs[:2], refs[2:4], refs[4:6], refs[6:]
    rows, width = fields[0].shape

    @pl.when(pl.program_id(0) == 0)
    def _():
        token = lax.broadcasted_iota(jnp.int32, (TILE, HEAD_DIM), 0)
        lane = lax.broadcasted_iota(jnp.int32, (TILE, HEAD_DIM), 1)
        part = part_ref[...]
        for i in range(rows // TILE):
            time_pos, band, column = (place_ref[3 * i + axis] for axis in range(3))
            row_pos = band * TILE_H + token // TILE_W
            col_pos = column * TILE_W + token % TILE_W
            position = jnp.where(part == 0, time_pos, jnp.where(part == 1, row_pos, col_pos))
            angles = position.astype(jnp.float32) * frequency_ref[...]
            cosine = jnp.cos(angles)
            sine = jnp.sin(angles) * jnp.where(lane % 2 == 0, -1.0, 1.0)
            at = slice(i * TILE, (i + 1) * TILE)
            for n, factor in enumerate((HEAD_DIM**-0.5 * math.log2(math.e), 1.0)):
                scale = lax.rsqrt(squares_ref[n : n + 1, at] / D + EPSILON) * factor
                scale = jnp.transpose(jnp.broadcast_to(scale, (TILE, HEAD_DIM)))
                tables[2 * n][at, :] = cosine * scale
                tables[2 * n + 1][at, :] = sine * scale

    row = lax.broadcasted_iota(jnp.int32, (HEAD_DIM, HEAD_DIM), 0)
    col = lax.broadcasted_iota(jnp.int32, (HEAD_DIM, HEAD_DIM), 1)
    exchange = (row == col + 1 - 2 * (col % 2)).astype(jnp.bfloat16)
    for n in range(2):
        for u in range(width // HEAD_DIM):
            cols = slice(u * HEAD_DIM, (u + 1) * HEAD_DIM)
            x = fields[n][:, cols]
            gain = jnp.broadcast_to(gains[n][:, cols], (8, HEAD_DIM))
            swapped = jnp.dot(x, exchange, preferred_element_type=jnp.float32)
            turned = (x.astype(jnp.float32) * gain[:1]) * tables[2 * n][...]
            turned += (swapped * exchange_pairs(gain)[:1]) * tables[2 * n + 1][...]
            outs[n][:, cols] = turned.astype(jnp.bfloat16)


def turn(place, squares, queries, keys, query_gain, key_gain):
    rows, width = queries.shape
    heads = width // HEAD_DIM
    step = 2 - heads % 2
    part, frequency = lane_tables()
    column = pl.BlockSpec((rows, step * HEAD_DIM), lambda h, place: (0, h))
    line = pl.BlockSpec((1, step * HEAD_DIM), lambda h, place: (0, h))
    lanes = pl.BlockSpec((1, HEAD_DIM), lambda h, place: (0, 0))
    whole = pl.BlockSpec((2, rows), lambda h, place: (0, 0))
    return pl.pallas_call(
        turn_kernel,
        grid_spec=pltpu.PrefetchScalarGridSpec(
            num_scalar_prefetch=1,
            grid=(heads // step,),
            in_specs=[lanes, lanes, whole, column, column, line, line],
            out_specs=[column, column],
            scratch_shapes=[pltpu.VMEM((rows, HEAD_DIM), jnp.float32) for _ in range(4)],
        ),
        out_shape=[jax.ShapeDtypeStruct((rows, width), jnp.bfloat16)] * 2,
        compiler_params=pltpu.CompilerParams(vmem_limit_bytes=24 * 2**20),
        cost_estimate=SMALL,
    )(
        place,
        part,
        frequency,
        squares,
        queries,
        keys,
        query_gain.reshape(1, width),
        key_gain.reshape(1, width),
    )


def choose_kernel(owner_ref, keys_ref, values_ref, o_ref):
    o_ref[0] = keys_ref[...]
    o_ref[1] = values_ref[...]


def choose(owner, text_keys, text_values):
    panels, rows, width = text_keys.shape
    samples = owner.shape[0]
    panel = pl.BlockSpec((None, rows, width), lambda s, owner: (owner[s], 0, 0))
    return pl.pallas_call(
        choose_kernel,
        grid_spec=pltpu.PrefetchScalarGridSpec(
            num_scalar_prefetch=1,
            grid=(samples,),
            in_specs=[panel, panel],
            out_specs=pl.BlockSpec((2, None, rows, width), lambda s, owner: (0, s, 0, 0)),
        ),
        out_shape=jax.ShapeDtypeStruct((2, samples, rows, width), text_keys.dtype),
        cost_estimate=SMALL,
    )(owner, text_keys, text_values)


def attend_blocks(heads, tiles, query, keys, bias, val_ref, s_ref, p_ref, floor_of, finish):
    def score(u, i):
        rows = slice(i * TILE, (i + 1) * TILE)
        s_ref[u, rows, :] = lax.dot_general(
            query(u, rows),
            keys(u),
            (((1,), (1,)), ((), ())),
            preferred_element_type=jnp.float32,
        )

    def weigh(u, i):
        rows = slice(i * TILE, (i + 1) * TILE)
        largest = None
        for j in range(s_ref.shape[2] // TILE):
            part = s_ref[u, rows, j * TILE : (j + 1) * TILE]
            if j < len(bias[i]):
                part = part + bias[i][j]
            largest = part if largest is None else jnp.maximum(largest, part)
        largest = jnp.max(largest, axis=1, keepdims=True)
        floor = floor_of(u, rows)
        if floor is None:
            largest = jnp.broadcast_to(largest, (TILE, HEAD_DIM))
        else:
            largest = jnp.maximum(largest, floor)
        for j in range(s_ref.shape[2] // TILE):
            cols = slice(j * TILE, (j + 1) * TILE)
            top = largest - bias[i][j] if j < len(bias[i]) else largest
            p_ref[u, rows, cols] = jnp.exp2(s_ref[u, rows, cols] - top).astype(jnp.bfloat16)
        return largest

    def mix(u, i, largest):
        rows = slice(i * TILE, (i + 1) * TILE)
        sums = jnp.dot(p_ref[u, rows, :], val_ref[u], preferred_element_type=jnp.float32)
        finish(u, rows, sums, largest)

    blocks = [(u, i) for i in range(tiles) for u in range(heads)]
    score(*blocks[0])
    score(*blocks[1])
    waiting = None
    for at, block in enumerate(blocks):
        if at + 2 < len(blocks):
            score(*blocks[at + 2])
        largest = weigh(*block)
        if waiting is not None:
            mix(*waiting)
        waiting = (*block, largest)
    mix(*waiting)


def bias_of(meta_ref, at, tiles):
    return [jnp.where(meta_ref[at + j] == 0, OUT_OF_WINDOW, 0.0) for j in range(tiles)]


def head_cols(u):
    return slice(u * HEAD_DIM, (u + 1) * HEAD_DIM)


def ones_once(val_ref):
    @pl.when(pl.program_id(0) == 0)
    def _():
        for u in range(val_ref.shape[0]):
            val_ref[u, :, HEAD_DIM:] = jnp.ones(val_ref.shape[1:2] + (HEAD_DIM,), jnp.bfloat16)


def own_kernel(meta_ref, q_ref, k_ref, v_ref, *rest):
    o_ref, val_ref, s_ref, p_ref = rest[-4:]
    tiles = k_ref.shape[0] // TILE
    heads = val_ref.shape[0]
    ones_once(val_ref)
    for u in range(heads):
        val_ref[u, :, :HEAD_DIM] = v_ref[:, head_cols(u)]

    def finish(u, rows, sums, largest):
        weight = sums[:, HEAD_DIM:]
        o_ref[rows, head_cols(2 * u)] = sums[:, :HEAD_DIM] / weight
        o_ref[rows, head_cols(2 * u + 1)] = largest + jnp.log2(weight)

    attend_blocks(
        heads,
        tiles,
        lambda u, rows: q_ref[rows, head_cols(u)],
        lambda u: k_ref[:, head_cols(u)],
        [bias_of(meta_ref, i * tiles, tiles) for i in range(tiles)],
        val_ref,
        s_ref,
        p_ref,
        lambda u, rows: None,
        finish,
    )


def attend_own(flags, q_hat, k_hat, values, first, heads, out=None):
    rows, width = q_hat.shape
    step = 1 if heads % 2 or first % 2 else 2
    wide = step * HEAD_DIM
    column = pl.BlockSpec((rows, wide), lambda h, flags: (0, first // step + h))
    operands, in_specs, aliases = [q_hat, k_hat, values], [column] * 3, {}
    if out is not None:
        in_specs.append(pl.BlockSpec(memory_space=pl.ANY))
        operands.append(out)
        aliases = {len(operands): 0}
    return pl.pallas_call(
        own_kernel,
        grid_spec=pltpu.PrefetchScalarGridSpec(
            num_scalar_prefetch=1,
            grid=(heads // step,),
            in_specs=in_specs,
            out_specs=pl.BlockSpec((rows, 2 * wide), lambda h, flags: (0, first // step + h)),
            scratch_shapes=[
                pltpu.VMEM((step, rows, 2 * HEAD_DIM), jnp.bfloat16),
                pltpu.VMEM((step, rows, rows), jnp.float32),
                pltpu.VMEM((step, rows, rows), jnp.bfloat16),
            ],
        ),
        out_shape=jax.ShapeDtypeStruct((rows, 2 * width), jnp.float32),
        input_output_aliases=aliases,
        compiler_params=pltpu.CompilerParams(vmem_limit_bytes=40 * 2**20),
        cost_estimate=cost(heads, rows, rows),
    )(flags, *operands)


def rest_kernel(shards, meta_ref, q_ref, part_ref, kn_ref, vn_ref, *rest):
    text_refs = rest[:shards]
    o_ref, key_ref, val_ref, s_ref, p_ref = rest[-5:]
    near = kn_ref.shape[0]
    heads = val_ref.shape[0]
    ones_once(val_ref)
    for u in range(heads):
        cols = head_cols(u)
        key_ref[u, :near, :] = kn_ref[:, cols]
        val_ref[u, :near, :HEAD_DIM] = vn_ref[:, cols]
        at = near
        for text_ref in text_refs:
            rows = slice(at, at + text_ref.shape[1])
            key_ref[u, rows, :] = text_ref[0, :, cols]
            val_ref[u, rows, :HEAD_DIM] = text_ref[1, :, cols]
            at += text_ref.shape[1]

    def floor_of(u, rows):
        return part_ref[rows, head_cols(2 * u + 1)]

    def finish(u, rows, sums, largest):
        kept = jnp.exp2(floor_of(u, rows) - largest)
        summed = sums[:, :HEAD_DIM] + kept * part_ref[rows, head_cols(2 * u)]
        o_ref[rows, head_cols(u)] = (summed / (sums[:, HEAD_DIM:] + kept)).astype(jnp.bfloat16)

    near_tiles = near // TILE
    attend_blocks(
        heads,
        FRAME_TILES,
        lambda u, rows: q_ref[rows, head_cols(u)],
        lambda u: key_ref[u],
        [bias_of(meta_ref, 2 + i * near_tiles, near_tiles) for i in range(FRAME_TILES)],
        val_ref,
        s_ref,
        p_ref,
        floor_of,
        finish,
    )


def attend_rest(meta, q_hat, part, near_k, near_v, shards, first, heads, out=None):
    rows, width = q_hat.shape
    total = FRAME + TXT
    step = 1 if heads % 2 or first % 2 else 2
    wide = step * HEAD_DIM
    frame_block = pl.BlockSpec((FRAME, wide), lambda h, meta: (meta[0], first // step + h))
    in_specs = [
        frame_block,
        pl.BlockSpec((FRAME, 2 * wide), lambda h, meta: (meta[0], first // step + h)),
        pl.BlockSpec((None, FRAME, wide), lambda h, meta: (0, 0, h)),
        pl.BlockSpec((None, FRAME, wide), lambda h, meta: (near_v.shape[0] - 1, 0, h)),
    ] + [
        pl.BlockSpec(
            (2, None, shard.shape[2], wide), lambda h, meta: (0, meta[1], 0, first // step + h)
        )
        for shard in shards
    ]
    operands = [q_hat, part, near_k, near_v, *shards]
    aliases = {}
    if out is not None:
        in_specs.append(pl.BlockSpec(memory_space=pl.ANY))
        operands.append(out)
        aliases = {len(operands): 0}
    return pl.pallas_call(
        functools.partial(rest_kernel, len(shards)),
        grid_spec=pltpu.PrefetchScalarGridSpec(
            num_scalar_prefetch=1,
            grid=(heads // step,),
            in_specs=in_specs,
            out_specs=frame_block,
            scratch_shapes=[
                pltpu.VMEM((step, total, HEAD_DIM), jnp.bfloat16),
                pltpu.VMEM((step, total, 2 * HEAD_DIM), jnp.bfloat16),
                pltpu.VMEM((step, FRAME, total), jnp.float32),
                pltpu.VMEM((step, FRAME, total), jnp.bfloat16),
            ],
        ),
        out_shape=jax.ShapeDtypeStruct((rows, width), jnp.bfloat16),
        input_output_aliases=aliases,
        compiler_params=pltpu.CompilerParams(vmem_limit_bytes=32 * 2**20),
        cost_estimate=cost(heads, FRAME, total),
    )(meta, *operands)


def side_route(count, level):
    last = count // 2 - 1
    first, second, is_straight = [], [], [False] * count
    for k in range(last):
        low, high = 2 * k + 1, 2 * k + 2
        for source, target, relays in ((low, high, k < level), (high, low, k >= last - level)):
            if relays:
                first.append((source, source ^ 1))
                second.append((source ^ 1, target))
            else:
                first.append((source, target))
                is_straight[target] = True
    return first, second, is_straight


def after(value, *others):
    return lax.optimization_barrier((value, *others))[0]


def local(
    queries, keys, values, query_gain, key_gain, shapes, windows, text_keys, text_values, owner
):
    rows, width = queries.shape
    heads = width // HEAD_DIM
    count = lax.axis_size("seq")
    me = lax.axis_index("seq")
    odd = me % 2
    pair = [(i, i ^ 1) for i in range(count)]
    pair_frame, side_frame = 1 - odd, odd

    chosen = choose(owner, text_keys, text_values)
    both = jnp.concatenate([chosen, lax.ppermute(chosen, "seq", pair)], axis=2)
    pair_values = lax.dynamic_slice_in_dim(after(values, chosen), pair_frame * FRAME, FRAME, 0)
    near_values = lax.ppermute(pair_values[None], "seq", pair)
    if count <= 8:
        shards = [both] + [
            lax.ppermute(both, "seq", [(i, (i + 2 * k) % count) for i in range(count)])
            for k in range(count // 2 - 1, 0, -1)
        ]
    else:
        groups = [list(range(start, count, 2)) for start in range(2)]
        shards = [lax.all_gather(both, "seq", axis=2, tiled=True, axis_index_groups=groups)]

    place, own_flags, pair_meta, side_meta = plan(me, shapes, windows)
    query_wide, key_wide, _ = lax.optimization_barrier((queries, keys, chosen))
    query_wide = query_wide.astype(jnp.float32)
    key_wide = key_wide.astype(jnp.float32)
    squares = head_sum(
        jnp.stack([jnp.sum(query_wide * query_wide, axis=1), jnp.sum(key_wide * key_wide, axis=1)])
    )
    q_hat, k_hat = turn(place, squares, queries, keys, query_gain, key_gain)
    pair_keys = lax.dynamic_slice_in_dim(k_hat, pair_frame * FRAME, FRAME, 0)[None]
    near_keys = lax.ppermute(pair_keys, "seq", pair)
    part = attend_own(own_flags, q_hat, k_hat, values, 0, heads)
    out = attend_rest(pair_meta, q_hat, part, near_keys, near_values, shards, 0, heads)

    few = max(1, heads * 2 // 5)
    relays = count // 2 - 1 if count == 8 else 0
    parcels = (
        (few, relays, (near_values,)),
        (heads - few, 0, (near_keys, part, *shards)),
    )
    side_keys = lax.dynamic_slice_in_dim(k_hat, side_frame * FRAME, FRAME, 0)
    side_values = lax.dynamic_slice_in_dim(values, side_frame * FRAME, FRAME, 0)
    side_parcels = []
    start = 0
    for step, level, gate in parcels:
        cols = slice(start * HEAD_DIM, (start + step) * HEAD_DIM)
        parcel = jnp.stack([side_keys[:, cols], side_values[:, cols]])
        straight, relayed, is_straight = side_route(count, level)
        arrived = lax.ppermute(after(parcel, *gate), "seq", straight)
        if relayed:
            forwarded = lax.ppermute(arrived, "seq", relayed)
            if any(is_straight):
                forwarded = jnp.where(jnp.asarray(is_straight)[me], arrived, forwarded)
            arrived = forwarded
        side_parcels.append(arrived)
        start += step
    start = 0
    for (step, *_), parcel in zip(parcels, side_parcels):
        out = attend_rest(side_meta, q_hat, part, parcel, parcel, shards, start, step, out)
        start += step
    return out


def solution(mesh):
    placed = (
        P("seq", "head"),
        P("seq", "head"),
        P("seq", "head"),
        P("head"),
        P("head"),
        P(),
        P("seq", None),
        P(None, "seq", "head"),
        P(None, "seq", "head"),
        P(),
    )
    return jax.shard_map(
        local, mesh=mesh, in_specs=placed, out_specs=P("seq", "head"), check_vma=False
    )
```
